256 devices in a mesh: gy: 32 (over x, y, core), gz: 8 (over z).
Axes of the slice: x: 4, y: 4, z: 8, core: 2. Of those that a mesh axis runs over, the one named last changes fastest.
Arguments:
- field: float32 [10, 512, 32, 4096], P(None, 'gz', None, 'gy'), may hold values from -6 to 6
- tf_density: float32 [8], replicated, may hold values from 0.1 to 3
- tf_color: float32 [3, 8], replicated, may hold values from 0.1 to 1
Outputs:
- image: float32 [10, 4, 32, 4096], P(None, None, 'gz', 'gy')
The draws below stay inside these ranges and needn't reach their ends.
All inputs are finite; a program needn't handle non-finite values.
Results may differ from the reference program's by a relative error of at most 0.000058.
Values sent between devices are 32-bit elements; how exact they have to be, the bound alone decides.
No kernel may reach another device: no remote copies, remote signals or barrier semaphores. Data moves between devices by JAX's collectives and lax.ppermute only.
A program may use at most 128 MiB of HBM per device.

```python
import math
import jax
import jax.numpy as jnp
from jax import lax

NX = 32
KB = 8
F = 10
NZ = 512
NY = 4096


def level_of(key, extent, cuts, least, high):
    def one(position, blocks):
        draws = jax.random.uniform(jax.random.fold_in(jax.random.fold_in(key, 6), position), (blocks,), jnp.float32, least / len(cuts), high / len(cuts))
        return jnp.repeat(jnp.exp(draws), extent[position] // blocks).reshape((-1,) + (1,) * (len(extent) - position - 1))

    level = one(*cuts[0])
    for cut in cuts[1:]:
        level = level * one(*cut)
    return level


def scatter_about(own_key, extent, scale, reach, shards=(), dtype=jnp.bfloat16):
    loudness = level_of(own_key, extent, shards, -0.22, 0.18) if shards else 1.0
    entries = jax.random.normal(own_key, extent, jnp.float32) * scale * loudness
    return jnp.minimum(jnp.maximum(entries, -reach), reach).astype(dtype)


def setup_inputs(seed: int = 0) -> dict:
    key_of = jax.random.split(jax.random.key(seed), 4)
    field = scatter_about(key_of[0], (F, NZ, NX, NY), 1.0, 6.0, ((1, 8), (3, 32)), jnp.float32)
    tf_density = jnp.clip(jnp.exp(jax.random.uniform(key_of[1], (KB,), jnp.float32, math.log(0.1), math.log(3.0))), 0.1, 3.0)
    tf_color = jnp.clip(jax.random.uniform(key_of[2], (3, KB), jnp.float32, 0.1, 1.0), 0.1, 1.0)
    return {"field": field, "tf_density": tf_density, "tf_color": tf_color}


def render(volume, tf_density, tf_color):
    depth = volume.shape[0]
    padded = jnp.pad(volume, 1)
    grad_z = 0.5 * (padded[2:, 1:-1, 1:-1] - padded[:-2, 1:-1, 1:-1])
    grad_x = 0.5 * (padded[1:-1, 2:, 1:-1] - padded[1:-1, :-2, 1:-1])
    grad_y = 0.5 * (padded[1:-1, 1:-1, 2:] - padded[1:-1, 1:-1, :-2])
    lit = 0.3 + 0.7 * jnp.abs(0.6 * grad_z + 0.48 * grad_x + 0.64 * grad_y) / jnp.sqrt(grad_z * grad_z + grad_x * grad_x + grad_y * grad_y + 1.0)
    count = tf_density.shape[0]
    step = 1.5 / depth
    tau = jnp.zeros(volume.shape, jnp.float32)
    tints = [jnp.zeros(volume.shape, jnp.float32) for channel in range(3)]
    for index in range(count):
        center = -2.0 + 4.0 * index / (count - 1)
        bump = jnp.exp(-2.0 * (volume - center) ** 2)
        tau = tau + tf_density[index] * bump
        tints = [tints[c] + tf_color[c, index] * bump for c in range(3)]
    tau = step * tau
    ahead = jnp.cumsum(tau, axis=0) - tau
    weight = jnp.exp(-ahead) * (1.0 - jnp.exp(-tau)) * lit
    colors = [lax.optimization_barrier(jnp.sum(weight * tints[c], axis=0)) for c in range(3)]
    opacity = 1.0 - jnp.exp(-lax.optimization_barrier(jnp.sum(tau, axis=0)))
    return jnp.stack(colors + [opacity], axis=0)

def reference(field, tf_density, tf_color):
    return lax.map(lambda volume: render(volume, tf_density, tf_color), field)
```

```python
import functools
import math

import jax
import jax.numpy as jnp
from jax import lax
from jax.experimental import pallas as pl
from jax.experimental.pallas import tpu as pltpu
from jax.sharding import PartitionSpec as P

BUMPS = 8
BASE = 3
SPACING = 4.0 / (BUMPS - 1)
CENTRE = -2.0 + SPACING * BASE
LOG2E = math.log2(math.e)
RATE = 4.0 * SPACING * LOG2E
BELL = -2.0 * LOG2E / (RATE * RATE)
FALL = [math.exp(-2.0 * ((j - BASE) * SPACING) ** 2) for j in range(BUMPS)]
LANES = 128
TILE = 8
PITCH = 40


def edges_kernel(odd_ref, field_ref, outer_ref, second_ref, pair_ref, next_ref, cells, sems):
    frames, depth, columns = field_ref.shape[:3]
    lane = lax.broadcasted_iota(jnp.int32, (TILE, LANES), 1)
    odd_z = odd_ref[1] == 1
    spans = [slice(t, t + TILE) for t in range(0, columns, TILE)]

    def load(f):
        return pltpu.make_async_copy(field_ref.at[f], cells.at[f], sems.at[f])

    for f in range(frames):
        load(f).start()

    def one_frame(f, _):
        load(f).wait()
        outer = [jnp.zeros((TILE, LANES), jnp.float32) for _ in spans]
        second = [jnp.zeros((TILE, LANES), jnp.float32) for _ in spans]
        for z in range(depth):
            own = (lane >> 1) == z
            near = (lane == (2 * z - 1) % LANES) | (lane == (2 * z + 2) % LANES)
            for t, span in enumerate(spans):
                turned = pltpu.roll(cells[f, z, span, :], (2 * z + 1) % LANES, 1)
                outer[t] = jnp.where(own, turned, outer[t])
                second[t] = jnp.where(near, turned, second[t])
        for t, span in enumerate(spans):
            outer_ref[f, span, :] = outer[t]
            second_ref[f, span, :] = second[t]
            front, back = cells[f, 0, span, :], cells[f, depth - 1, span, :]
            pair_ref[f, span, :] = jnp.where(odd_z, front, back)
            next_ref[f, span, :] = jnp.where(odd_z, back, front)
        return 0

    lax.fori_loop(0, frames, one_frame, 0)


def render_kernel(
    odd_ref,
    density_ref,
    color_ref,
    z1_ref,
    z2_ref,
    y1_ref,
    y2_ref,
    second_ref,
    field_ref,
    *rest,
    step,
    start,
):
    kept_ref, sent_ref, cells, sems = rest[-4:]
    frame, frames = pl.program_id(0), pl.num_programs(0)
    depth, columns = field_ref.shape[1], field_ref.shape[2]
    tiles = columns // TILE
    slot = lax.rem(frame, 2)

    def load(which, into):
        return pltpu.make_async_copy(
            field_ref.at[start + which], cells.at[into, pl.ds(1, depth), pl.ds(TILE, columns), :], sems.at[into]
        )

    @pl.when(frame == 0)
    def _():
        load(0, 0).start()
        for into in range(2):
            for plane in range(depth + 3):
                cells[into, plane, 0:TILE, :] = jnp.zeros((TILE, LANES), jnp.float32)

    @pl.when(frame + 1 < frames)
    def _():
        load(frame + 1, 1 - slot).start()

    odd_y, odd_z, late = odd_ref[0] == 1, odd_ref[1] == 1, odd_ref[2]
    lane = lax.broadcasted_iota(jnp.int32, (TILE, LANES), 1)
    even_lane = (lane & 1) == 0
    edge_lane = (lane == 0) | (lane == LANES - 1)

    rows = cells.reshape(2 * cells.shape[1] * PITCH, LANES)
    first = slot * (cells.shape[1] * PITCH) + TILE

    for t in range(tiles):
        here = slice(t * TILE, (t + 1) * TILE)
        a, b = z1_ref[0, here, :], z2_ref[0, here, :]
        cells[slot, 0, TILE + t * TILE : TILE + (t + 1) * TILE, :] = jnp.where(odd_z, a, b)
        cells[slot, depth + 1, TILE + t * TILE : TILE + (t + 1) * TILE, :] = jnp.where(odd_z, b, a)

    scale = [-LOG2E * step * FALL[j] for j in range(BUMPS)]
    dens = [jnp.full((TILE, LANES), density_ref[j] * scale[j], jnp.float32) for j in range(BUMPS)]
    load(frame, slot).wait()

    def one_tile(t, _):
        top = first + t * TILE
        here = pl.ds(pl.multiple_of(t * TILE, TILE), TILE)
        a, b = y1_ref[0, here, :], y2_ref[0, here, :]
        left, right = jnp.where(odd_y, a, b), jnp.where(odd_y, b, a)
        second = second_ref[0, here, :]
        rim = jnp.where(
            even_lane,
            pltpu.roll(right, LANES - 1, 1) - pltpu.roll(second, 1, 1),
            pltpu.roll(second, LANES - 1, 1) - pltpu.roll(left, 1, 1),
        )

        def one_depth(z, carry):
            total, clear, before, cell = carry[:4]
            sums = list(carry[4:])
            row = top + (z + 1) * PITCH
            after = rows[pl.ds(pl.multiple_of(row + PITCH, TILE), TILE), :]
            gz = after - before
            gx = rows[pl.ds(row + 1, TILE), :] - rows[pl.ds(row - 1, TILE), :]
            gy = pltpu.roll(cell, LANES - 1, 1) - pltpu.roll(cell, 1, 1)
            gy = jnp.where(edge_lane, pltpu.roll(rim, LANES - 1 - 2 * z, 1), gy)
            slope = jnp.abs(gz + 0.8 * gx + (16.0 / 15.0) * gy)
            lit = (0.3 / 0.42) + slope * lax.rsqrt(gz * gz + gx * gx + gy * gy + 4.0)
            q = cell * RATE - (CENTRE * RATE)
            up = jnp.exp2(q)
            down = jnp.exp2(-q)
            bell = jnp.exp2(q * q * BELL)
            high = (((dens[7] * up + dens[6]) * up + dens[5]) * up + dens[4]) * up + dens[3]
            low = ((dens[0] * down + dens[1]) * down + dens[2]) * down
            total = total + (high + low) * bell
            behind = jnp.exp2(total)
            power = (clear - behind) * lit * bell
            sums[BASE] = sums[BASE] + power
            rise = power
            for j in range(BASE + 1, BUMPS):
                rise = rise * up
                sums[j] = sums[j] + rise
            drop = power
            for j in range(BASE - 1, -1, -1):
                drop = drop * down
                sums[j] = sums[j] + drop
            return (total, behind, cell, after, *sums)

        zero = jnp.zeros((TILE, LANES), jnp.float32)
        begin = (
            zero,
            zero + 1.0,
            rows[pl.ds(pl.multiple_of(top, TILE), TILE), :],
            rows[pl.ds(pl.multiple_of(top + PITCH, TILE), TILE), :],
        ) + (zero,) * BUMPS
        final = begin
        for z in range(depth):
            final = one_depth(z, final)
        total, sums = final[0], final[4:]
        parts = []
        for c in range(3):
            parts.append(
                functools.reduce(
                    jnp.add, [(color_ref[c, j] * (0.42 * FALL[j])) * sums[j] for j in range(BUMPS)]
                )
            )
        parts.append(total)
        keep_first = late == jnp.where(t >= 2, 1, 0)
        share = jnp.where(t == 0, 0, jnp.where(t == 1, 2, jnp.where(t == 2, 3, 1)))
        for c in range(4):
            kept_ref[share, 0, c, :, :] = jnp.where(keep_first, parts[c][0:4], parts[c][4:8])
            sent_ref[share, 0, c, :, :] = jnp.where(keep_first, parts[c][4:8], parts[c][0:4])
        return 0

    lax.fori_loop(0, tiles, one_tile, 0)


def joined(kept, arrived, in_front):
    front, back = jnp.where(in_front, kept, arrived), jnp.where(in_front, arrived, kept)
    clear = jnp.exp2(front[:, :, 3:4])
    return jnp.concatenate([front[:, :, :3] + clear * back[:, :, :3], front[:, :, 3:] + back[:, :, 3:]], axis=2)


def halves(value, late):
    half = value.shape[0] // 2
    kept = jnp.where(late == 0, value[:half], value[half:])
    return kept, jnp.where(late == 0, value[half:], value[:half])


def pairs_of(count, offset):
    lows = range(offset, count - 1, 2)
    return [(i, i + 1) for i in lows] + [(i + 1, i) for i in lows]


def local(field, tf_density, tf_color):
    frames, depth, columns, rows = field.shape
    ny, nz = lax.axis_size("gy"), lax.axis_size("gz")
    step = 1.5 / (depth * nz)
    place = lax.axis_index("gz")
    quarter = jnp.where(place < nz // 2, place, nz - 1 - place)
    odd = jnp.stack([lax.axis_index("gy") % 2, place % 2, quarter % 2]).astype(jnp.int32)
    split = 7

    smem = pl.BlockSpec(memory_space=pltpu.SMEM)
    anywhere, vmem = pl.BlockSpec(memory_space=pl.ANY), pl.BlockSpec(memory_space=pltpu.VMEM)
    plane = jax.ShapeDtypeStruct((frames, columns, rows), jnp.float32)
    outer, second, pair, other = pl.pallas_call(
        edges_kernel,
        in_specs=[smem, anywhere],
        out_specs=[vmem] * 4,
        out_shape=[plane] * 4,
        scratch_shapes=[pltpu.VMEM(field.shape, jnp.float32), pltpu.SemaphoreType.DMA((frames,))],
        compiler_params=pltpu.CompilerParams(vmem_limit_bytes=56 * 2**20),
        name="edges",
    )(odd, field)
    z1 = lax.ppermute(pair, "gz", pairs_of(nz, 0))
    z2 = lax.ppermute(other, "gz", pairs_of(nz, 1))
    y1 = lax.ppermute(outer, "gy", pairs_of(ny, 0))
    y2 = lax.ppermute(outer, "gy", pairs_of(ny, 1))

    def render(name, start, count, *earlier):
        voxels = count * depth * columns * rows
        share = jax.ShapeDtypeStruct((4, count, 4, columns // nz, rows), jnp.float32)
        share_spec = pl.BlockSpec((4, 1, 4, columns // nz, rows), lambda f: (0, f, 0, 0, 0))
        plane_spec = pl.BlockSpec((1, columns, rows), lambda f: (f + start, 0, 0))
        return pl.pallas_call(
            functools.partial(render_kernel, step=step, start=start),
            grid=(count,),
            in_specs=[smem, smem, smem] + [plane_spec] * 5 + [anywhere] * (1 + len(earlier)),
            out_specs=[share_spec, share_spec],
            out_shape=[share, share],
            scratch_shapes=[
                pltpu.VMEM((2, depth + 3, PITCH, LANES), jnp.float32),
                pltpu.SemaphoreType.DMA((2,)),
            ],
            compiler_params=pltpu.CompilerParams(vmem_limit_bytes=52 * 2**20),
            cost_estimate=pl.CostEstimate(flops=12000 * voxels, bytes_accessed=4 * voxels, transcendentals=5 * voxels),
            name=name,
        )(odd, tf_density, tf_color, z1, z2, y1, y2, second, field, *earlier)

    def swapped(value, partner):
        return lax.ppermute(value, "gz", [(i, partner(i)) for i in range(nz)])

    def swapped_first(sent):
        return swapped(sent, lambda i: i ^ 1)

    kept_a, sent_a = render("render_a", 0, split)
    kept_b, sent_b = render("render_b", split, frames - split, kept_a)
    arrived_a, sent_b = lax.optimization_barrier((swapped_first(sent_a), sent_b))
    in_front = place % 2 == 0
    value = jnp.concatenate(
        [joined(kept_a, arrived_a, in_front), joined(kept_b, swapped_first(sent_b), in_front)], axis=1
    )
    kept, sent = halves(value, quarter // 2)
    value = joined(kept, swapped(sent, lambda i: i ^ 2), place // 2 % 2 == 0)
    kept, sent = halves(value, place // 4)
    value = joined(kept, swapped(sent, lambda i: nz - 1 - i), place < nz // 2)[0]
    return jnp.concatenate([value[:, :3], 1.0 - jnp.exp2(value[:, 3:])], axis=1)


def solution(mesh):
    placed = (P(None, "gz", None, "gy"), P(), P())
    return jax.shard_map(
        local, mesh=mesh, in_specs=placed, out_specs=P(None, None, "gz", "gy"), check_vma=False
    )
```

```python
import functools
import math

import jax
import jax.numpy as jnp
from jax import lax
from jax.experimental import pallas as pl
from jax.experimental.pallas import tpu as pltpu
from jax.sharding import PartitionSpec as P

BUMPS = 8
BASE = 3
SPACING = 4.0 / (BUMPS - 1)
CENTRE = -2.0 + SPACING * BASE
LOG2E = math.log2(math.e)
RATE = 4.0 * SPACING * LOG2E
BELL = -2.0 * LOG2E / (RATE * RATE)
FALL = [math.exp(-2.0 * ((j - BASE) * SPACING) ** 2) for j in range(BUMPS)]
LANES = 128
TILE = 8
PITCH = 40


def edges_kernel(field_ref, outer_ref, second_ref, pair_ref, next_ref, cells, sems):
    frames, depth, columns = field_ref.shape[:3]
    lane = lax.broadcasted_iota(jnp.int32, (TILE, LANES), 1)
    odd_z = lax.axis_index("gz") % 2 == 1
    spans = [slice(t, t + TILE) for t in range(0, columns, TILE)]

    def load(f):
        return pltpu.make_async_copy(field_ref.at[f], cells.at[f], sems.at[f])

    for f in range(frames):
        load(f).start()

    def one_frame(f, _):
        load(f).wait()
        outer = [jnp.zeros((TILE, LANES), jnp.float32) for _ in spans]
        second = [jnp.zeros((TILE, LANES), jnp.float32) for _ in spans]
        for z in range(depth):
            own = (lane >> 1) == z
            near = (lane == (2 * z - 1) % LANES) | (lane == (2 * z + 2) % LANES)
            for t, span in enumerate(spans):
                turned = pltpu.roll(cells[f, z, span, :], (2 * z + 1) % LANES, 1)
                outer[t] = jnp.where(own, turned, outer[t])
                second[t] = jnp.where(near, turned, second[t])
        for t, span in enumerate(spans):
            outer_ref[f, span, :] = outer[t]
            second_ref[f, span, :] = second[t]
            front, back = cells[f, 0, span, :], cells[f, depth - 1, span, :]
            pair_ref[f, span, :] = jnp.where(odd_z, front, back)
            next_ref[f, span, :] = jnp.where(odd_z, back, front)
        return 0

    lax.fori_loop(0, frames, one_frame, 0)


def quarter_of(place, count):
    return jnp.where(place < count // 2, place, count - 1 - place)


def render_kernel(
    density_ref,
    color_ref,
    z1_ref,
    z2_ref,
    y1_ref,
    y2_ref,
    second_ref,
    field_ref,
    *rest,
    step,
    start,
):
    kept_ref, sent_ref, cells, sems = rest[-4:]
    depth, columns = field_ref.shape[1], field_ref.shape[2]
    frames = kept_ref.shape[1]
    tiles = columns // TILE

    def load(frame, into, t):
        return pltpu.make_async_copy(
            field_ref.at[start + frame, :, pl.ds(t * TILE, TILE), :],
            cells.at[into, pl.ds(1, depth), pl.ds((t + 1) * TILE, TILE), :],
            sems.at[into, t],
        )

    for t in range(tiles):
        load(0, 0, t).start()
    for into in range(2):
        for plane in range(depth + 3):
            cells[into, plane, 0:TILE, :] = jnp.zeros((TILE, LANES), jnp.float32)

    place = lax.axis_index("gz")
    odd_y, odd_z, late = lax.axis_index("gy") % 2 == 1, place % 2 == 1, quarter_of(place, lax.axis_size("gz")) % 2
    lane = lax.broadcasted_iota(jnp.int32, (TILE, LANES), 1)
    even_lane = (lane & 1) == 0
    edge_lane = (lane == 0) | (lane == LANES - 1)
    rows = cells.reshape(2 * cells.shape[1] * PITCH, LANES)
    scale = [-LOG2E * step * FALL[j] for j in range(BUMPS)]
    dens = [jnp.full((TILE, LANES), density_ref[j] * scale[j], jnp.float32) for j in range(BUMPS)]

    def one_tile(frame, slot, t):
        top = slot * (cells.shape[1] * PITCH) + TILE + t * TILE
        here = pl.ds(pl.multiple_of(t * TILE, TILE), TILE)
        a, b = y1_ref[start + frame, here, :], y2_ref[start + frame, here, :]
        left, right = jnp.where(odd_y, a, b), jnp.where(odd_y, b, a)
        second = second_ref[start + frame, here, :]
        rim = jnp.where(
            even_lane,
            pltpu.roll(right, LANES - 1, 1) - pltpu.roll(second, 1, 1),
            pltpu.roll(second, LANES - 1, 1) - pltpu.roll(left, 1, 1),
        )

        def one_depth(z, carry):
            total, clear, before, cell = carry[:4]
            sums = list(carry[4:])
            row = top + (z + 1) * PITCH
            after = rows[pl.ds(pl.multiple_of(row + PITCH, TILE), TILE), :]
            gz = after - before
            gx = rows[pl.ds(row + 1, TILE), :] - rows[pl.ds(row - 1, TILE), :]
            gy = pltpu.roll(cell, LANES - 1, 1) - pltpu.roll(cell, 1, 1)
            gy = jnp.where(edge_lane, pltpu.roll(rim, LANES - 1 - 2 * z, 1), gy)
            slope = jnp.abs(gz + 0.8 * gx + (16.0 / 15.0) * gy)
            lit = (0.3 / 0.42) + slope * lax.rsqrt(gz * gz + gx * gx + gy * gy + 4.0)
            q = cell * RATE - (CENTRE * RATE)
            up = jnp.exp2(q)
            down = jnp.exp2(-q)
            bell = jnp.exp2(q * q * BELL)
            high = (((dens[7] * up + dens[6]) * up + dens[5]) * up + dens[4]) * up + dens[3]
            low = ((dens[0] * down + dens[1]) * down + dens[2]) * down
            total = total + (high + low) * bell
            behind = jnp.exp2(total)
            power = (clear - behind) * lit * bell
            sums[BASE] = sums[BASE] + power
            rise = power
            for j in range(BASE + 1, BUMPS):
                rise = rise * up
                sums[j] = sums[j] + rise
            drop = power
            for j in range(BASE - 1, -1, -1):
                drop = drop * down
                sums[j] = sums[j] + drop
            return (total, behind, cell, after, *sums)

        zero = jnp.zeros((TILE, LANES), jnp.float32)
        begin = (
            zero,
            zero + 1.0,
            rows[pl.ds(pl.multiple_of(top, TILE), TILE), :],
            rows[pl.ds(pl.multiple_of(top + PITCH, TILE), TILE), :],
        ) + (zero,) * BUMPS
        final = begin
        for z in range(depth):
            final = one_depth(z, final)
        total, sums = final[0], final[4:]
        parts = []
        for c in range(3):
            parts.append(
                functools.reduce(
                    jnp.add, [(color_ref[c, j] * (0.42 * FALL[j])) * sums[j] for j in range(BUMPS)]
                )
            )
        parts.append(total)
        keep_first = late == jnp.where(t >= 2, 1, 0)
        share = jnp.where(t == 0, 0, jnp.where(t == 1, 2, jnp.where(t == 2, 3, 1)))
        for c in range(4):
            kept_ref[share, frame, c, :, :] = jnp.where(keep_first, parts[c][0:4], parts[c][4:8])
            sent_ref[share, frame, c, :, :] = jnp.where(keep_first, parts[c][4:8], parts[c][0:4])

    def one_frame(frame, _):
        slot = lax.rem(frame, 2)

        @pl.when(frame + 1 < frames)
        def _():
            for t in range(tiles):
                load(frame + 1, 1 - slot, t).start()

        for t in range(tiles):
            here, there = slice(t * TILE, (t + 1) * TILE), slice((t + 1) * TILE, (t + 2) * TILE)
            a, b = z1_ref[start + frame, here, :], z2_ref[start + frame, here, :]
            cells[slot, 0, there, :] = jnp.where(odd_z, a, b)
            cells[slot, depth + 1, there, :] = jnp.where(odd_z, b, a)
        load(frame, slot, 0).wait()

        def with_next(t, _):
            @pl.when(t + 1 < tiles)
            def _():
                load(frame, slot, t + 1).wait()

            one_tile(frame, slot, t)
            return 0

        lax.fori_loop(0, tiles, with_next, 0)
        return 0

    lax.fori_loop(0, frames, one_frame, 0)


def joined(kept, arrived, in_front):
    front, back = jnp.where(in_front, kept, arrived), jnp.where(in_front, arrived, kept)
    clear = jnp.exp2(front[:, :, 3:4])
    return jnp.concatenate([front[:, :, :3] + clear * back[:, :, :3], front[:, :, 3:] + back[:, :, 3:]], axis=2)


def halves(value, late):
    half = value.shape[0] // 2
    kept = jnp.where(late == 0, value[:half], value[half:])
    return kept, jnp.where(late == 0, value[half:], value[:half])


def pairs_of(count, offset):
    lows = range(offset, count - 1, 2)
    return [(i, i + 1) for i in lows] + [(i + 1, i) for i in lows]


def local(field, tf_density, tf_color):
    frames, depth, columns, rows = field.shape
    ny, nz = lax.axis_size("gy"), lax.axis_size("gz")
    step = 1.5 / (depth * nz)
    place = lax.axis_index("gz")
    late = quarter_of(place, nz) // 2
    split = 7

    smem = pl.BlockSpec(memory_space=pltpu.SMEM)
    anywhere, vmem = pl.BlockSpec(memory_space=pl.ANY), pl.BlockSpec(memory_space=pltpu.VMEM)
    plane = jax.ShapeDtypeStruct((frames, columns, rows), jnp.float32)
    outer, second, pair, other = pl.pallas_call(
        edges_kernel,
        in_specs=[anywhere],
        out_specs=[vmem] * 4,
        out_shape=[plane] * 4,
        scratch_shapes=[pltpu.VMEM(field.shape, jnp.float32), pltpu.SemaphoreType.DMA((frames,))],
        compiler_params=pltpu.CompilerParams(vmem_limit_bytes=52 * 2**20),
        name="edges",
    )(field)
    z1 = lax.ppermute(pair, "gz", pairs_of(nz, 0))
    z2 = lax.ppermute(other, "gz", pairs_of(nz, 1))
    y1 = lax.ppermute(outer, "gy", pairs_of(ny, 0))
    y2 = lax.ppermute(outer, "gy", pairs_of(ny, 1))

    def render(name, start, count, *earlier):
        voxels = count * depth * columns * rows
        share = jax.ShapeDtypeStruct((4, count, 4, columns // nz, rows), jnp.float32)
        return pl.pallas_call(
            functools.partial(render_kernel, step=step, start=start),
            in_specs=[smem, smem] + [vmem] * 5 + [anywhere] * (1 + len(earlier)),
            out_specs=[vmem, vmem],
            out_shape=[share, share],
            scratch_shapes=[
                pltpu.VMEM((2, depth + 3, PITCH, LANES), jnp.float32),
                pltpu.SemaphoreType.DMA((2, columns // TILE)),
            ],
            compiler_params=pltpu.CompilerParams(vmem_limit_bytes=52 * 2**20),
            cost_estimate=pl.CostEstimate(flops=12000 * voxels, bytes_accessed=4 * voxels, transcendentals=5 * voxels),
            name=name,
        )(tf_density, tf_color, z1, z2, y1, y2, second, field, *earlier)

    def swapped(value, partner):
        return lax.ppermute(value, "gz", [(i, partner(i)) for i in range(nz)])

    def swapped_first(sent):
        return swapped(sent, lambda i: i ^ 1)

    kept_a, sent_a = render("render_a", 0, split)
    kept_b, sent_b = render("render_b", split, frames - split, kept_a)
    arrived_a, sent_b = lax.optimization_barrier((swapped_first(sent_a), sent_b))

    def second_join(kept, arrived):
        kept, sent = halves(joined(kept, arrived, place % 2 == 0), late)
        return joined(kept, swapped(sent, lambda i: i ^ 2), place // 2 % 2 == 0)

    value = jnp.concatenate([second_join(kept_a, arrived_a), second_join(kept_b, swapped_first(sent_b))], axis=1)
    kept, sent = halves(value, place // 4)
    value = joined(kept, swapped(sent, lambda i: nz - 1 - i), place < nz // 2)[0]
    return jnp.concatenate([value[:, :3], 1.0 - jnp.exp2(value[:, 3:])], axis=1)


def solution(mesh):
    placed = (P(None, "gz", None, "gy"), P(), P())
    return jax.shard_map(
        local, mesh=mesh, in_specs=placed, out_specs=P(None, None, "gz", "gy"), check_vma=False
    )
```

```python
import functools
import math

import jax
import jax.numpy as jnp
from jax import lax
from jax.experimental import pallas as pl
from jax.experimental.pallas import tpu as pltpu
from jax.sharding import PartitionSpec as P

BUMPS = 8
SPACING = 4.0 / (BUMPS - 1)
LOG2E = math.log2(math.e)
LIFT = 49.0
RATE = 4.0 * SPACING * LOG2E
BELL = -2.0 * LOG2E / (RATE * RATE)
LEAN = -8.0 * LOG2E / RATE
FALL = [math.exp(-2.0 * (-2.0 + SPACING * j) ** 2) * 2.0**-LIFT for j in range(BUMPS)]
LANES = 128
TILE = 8
PITCH = 40


def edges_kernel(field_ref, outer_ref, second_ref, pair_ref, next_ref, cells, sems):
    frames, depth, columns = field_ref.shape[:3]
    lane = lax.broadcasted_iota(jnp.int32, (TILE, LANES), 1)
    odd_z = lax.axis_index("gz") % 2 == 1
    spans = [slice(t, t + TILE) for t in range(0, columns, TILE)]

    def load(f):
        return pltpu.make_async_copy(field_ref.at[f], cells.at[f], sems.at[f])

    for f in range(frames):
        load(f).start()

    def one_frame(f, _):
        load(f).wait()
        outer = [jnp.zeros((TILE, LANES), jnp.float32) for _ in spans]
        second = [jnp.zeros((TILE, LANES), jnp.float32) for _ in spans]
        for z in range(depth):
            own = (lane >> 1) == z
            near = (lane == (2 * z - 1) % LANES) | (lane == (2 * z + 2) % LANES)
            for t, span in enumerate(spans):
                turned = pltpu.roll(cells[f, z, span, :], (2 * z + 1) % LANES, 1)
                outer[t] = jnp.where(own, turned, outer[t])
                second[t] = jnp.where(near, turned, second[t])
        for t, span in enumerate(spans):
            outer_ref[f, span, :] = outer[t]
            second_ref[f, span, :] = second[t]
            front, back = cells[f, 0, span, :], cells[f, depth - 1, span, :]
            pair_ref[f, span, :] = jnp.where(odd_z, front, back)
            next_ref[f, span, :] = jnp.where(odd_z, back, front)
        return 0

    lax.fori_loop(0, frames, one_frame, 0)


def quarter_of(place, count):
    return jnp.where(place < count // 2, place, count - 1 - place)


def render_kernel(
    density_ref,
    color_ref,
    z1_ref,
    z2_ref,
    y1_ref,
    y2_ref,
    second_ref,
    field_ref,
    *rest,
    step,
    start,
):
    kept_ref, sent_ref, cells, sems = rest[-4:]
    depth, columns = field_ref.shape[1], field_ref.shape[2]
    frames = kept_ref.shape[1]
    tiles = columns // TILE

    def load(frame, into, t):
        return pltpu.make_async_copy(
            field_ref.at[start + frame, :, pl.ds(t * TILE, TILE), :],
            cells.at[into, pl.ds(1, depth), pl.ds((t + 1) * TILE, TILE), :],
            sems.at[into, t],
        )

    for t in range(tiles):
        load(0, 0, t).start()
    for into in range(2):
        for plane in range(depth + 3):
            cells[into, plane, 0:TILE, :] = jnp.zeros((TILE, LANES), jnp.float32)

    place = lax.axis_index("gz")
    odd_y, odd_z, late = lax.axis_index("gy") % 2 == 1, place % 2 == 1, quarter_of(place, lax.axis_size("gz")) % 2
    lane = lax.broadcasted_iota(jnp.int32, (TILE, LANES), 1)
    even_lane = (lane & 1) == 0
    edge_lane = (lane == 0) | (lane == LANES - 1)
    rows = cells.reshape(2 * cells.shape[1] * PITCH, LANES)
    scale = [-LOG2E * step * FALL[j] for j in range(BUMPS)]
    dens = [jnp.full((TILE, LANES), density_ref[j] * scale[j], jnp.float32) for j in range(BUMPS)]

    def one_tile(frame, slot, t):
        top = slot * (cells.shape[1] * PITCH) + TILE + t * TILE
        here = pl.ds(pl.multiple_of(t * TILE, TILE), TILE)
        a, b = y1_ref[start + frame, here, :], y2_ref[start + frame, here, :]
        left, right = jnp.where(odd_y, a, b), jnp.where(odd_y, b, a)
        second = second_ref[start + frame, here, :]
        rim = jnp.where(
            even_lane,
            pltpu.roll(right, LANES - 1, 1) - pltpu.roll(second, 1, 1),
            pltpu.roll(second, LANES - 1, 1) - pltpu.roll(left, 1, 1),
        )

        def one_depth(z, carry):
            total, clear, before, cell = carry[:4]
            sums = list(carry[4:])
            row = top + (z + 1) * PITCH
            after = rows[pl.ds(pl.multiple_of(row + PITCH, TILE), TILE), :]
            gz = after - before
            gx = rows[pl.ds(row + 1, TILE), :] - rows[pl.ds(row - 1, TILE), :]
            gy = pltpu.roll(cell, LANES - 1, 1) - pltpu.roll(cell, 1, 1)
            gy = jnp.where(edge_lane, pltpu.roll(rim, LANES - 1 - 2 * z, 1), gy)
            slope = jnp.abs(gz + 0.8 * gx + (16.0 / 15.0) * gy)
            lit = (0.3 / 0.42) + slope * lax.rsqrt(gz * gz + gx * gx + gy * gy + 4.0)
            u = cell * RATE
            up = jnp.exp2(u)
            bell = jnp.exp2((u * BELL + LEAN) * u + LIFT)
            series = dens[BUMPS - 1]
            for j in range(BUMPS - 2, -1, -1):
                series = series * up + dens[j]
            total = total + series * bell
            behind = jnp.exp2(total)
            power = (clear - behind) * lit * bell
            sums[0] = sums[0] + power
            for j in range(1, BUMPS):
                power = power * up
                sums[j] = sums[j] + power
            return (total, behind, cell, after, *sums)

        zero = jnp.zeros((TILE, LANES), jnp.float32)
        begin = (
            zero,
            zero + 1.0,
            rows[pl.ds(pl.multiple_of(top, TILE), TILE), :],
            rows[pl.ds(pl.multiple_of(top + PITCH, TILE), TILE), :],
        ) + (zero,) * BUMPS
        final = begin
        for z in range(depth):
            final = one_depth(z, final)
        total, sums = final[0], final[4:]
        parts = []
        for c in range(3):
            parts.append(
                functools.reduce(
                    jnp.add, [(color_ref[c, j] * (0.42 * FALL[j])) * sums[j] for j in range(BUMPS)]
                )
            )
        parts.append(total)
        keep_first = late == jnp.where(t >= 2, 1, 0)
        share = jnp.where(t == 0, 0, jnp.where(t == 1, 2, jnp.where(t == 2, 3, 1)))
        for c in range(4):
            kept_ref[share, frame, c, :, :] = jnp.where(keep_first, parts[c][0:4], parts[c][4:8])
            sent_ref[share, frame, c, :, :] = jnp.where(keep_first, parts[c][4:8], parts[c][0:4])

    def one_frame(frame, _):
        slot = lax.rem(frame, 2)

        @pl.when(frame + 1 < frames)
        def _():
            for t in range(tiles):
                load(frame + 1, 1 - slot, t).start()

        for t in range(tiles):
            here, there = slice(t * TILE, (t + 1) * TILE), slice((t + 1) * TILE, (t + 2) * TILE)
            a, b = z1_ref[start + frame, here, :], z2_ref[start + frame, here, :]
            cells[slot, 0, there, :] = jnp.where(odd_z, a, b)
            cells[slot, depth + 1, there, :] = jnp.where(odd_z, b, a)
        load(frame, slot, 0).wait()

        def with_next(t, _):
            @pl.when(t + 1 < tiles)
            def _():
                load(frame, slot, t + 1).wait()

            one_tile(frame, slot, t)
            return 0

        lax.fori_loop(0, tiles, with_next, 0)
        return 0

    lax.fori_loop(0, frames, one_frame, 0)


def joined(kept, arrived, in_front):
    front, back = jnp.where(in_front, kept, arrived), jnp.where(in_front, arrived, kept)
    clear = jnp.exp2(front[:, :, 3:4])
    return jnp.concatenate([front[:, :, :3] + clear * back[:, :, :3], front[:, :, 3:] + back[:, :, 3:]], axis=2)


def halves(value, late):
    half = value.shape[0] // 2
    kept = jnp.where(late == 0, value[:half], value[half:])
    return kept, jnp.where(late == 0, value[half:], value[:half])


def pairs_of(count, offset):
    lows = range(offset, count - 1, 2)
    return [(i, i + 1) for i in lows] + [(i + 1, i) for i in lows]


def local(field, tf_density, tf_color):
    frames, depth, columns, rows = field.shape
    ny, nz = lax.axis_size("gy"), lax.axis_size("gz")
    step = 1.5 / (depth * nz)
    place = lax.axis_index("gz")
    late = quarter_of(place, nz) // 2
    split = 7

    smem = pl.BlockSpec(memory_space=pltpu.SMEM)
    anywhere, vmem = pl.BlockSpec(memory_space=pl.ANY), pl.BlockSpec(memory_space=pltpu.VMEM)
    plane = jax.ShapeDtypeStruct((frames, columns, rows), jnp.float32)
    outer, second, pair, other = pl.pallas_call(
        edges_kernel,
        in_specs=[anywhere],
        out_specs=[vmem] * 4,
        out_shape=[plane] * 4,
        scratch_shapes=[pltpu.VMEM(field.shape, jnp.float32), pltpu.SemaphoreType.DMA((frames,))],
        compiler_params=pltpu.CompilerParams(vmem_limit_bytes=52 * 2**20),
        name="edges",
    )(field)
    z1 = lax.ppermute(pair, "gz", pairs_of(nz, 0))
    z2 = lax.ppermute(other, "gz", pairs_of(nz, 1))
    y1 = lax.ppermute(outer, "gy", pairs_of(ny, 0))
    y2 = lax.ppermute(outer, "gy", pairs_of(ny, 1))

    def render(name, start, count, *earlier):
        voxels = count * depth * columns * rows
        share = jax.ShapeDtypeStruct((4, count, 4, columns // nz, rows), jnp.float32)
        return pl.pallas_call(
            functools.partial(render_kernel, step=step, start=start),
            in_specs=[smem, smem] + [vmem] * 5 + [anywhere] * (1 + len(earlier)),
            out_specs=[vmem, vmem],
            out_shape=[share, share],
            scratch_shapes=[
                pltpu.VMEM((2, depth + 3, PITCH, LANES), jnp.float32),
                pltpu.SemaphoreType.DMA((2, columns // TILE)),
            ],
            compiler_params=pltpu.CompilerParams(vmem_limit_bytes=52 * 2**20),
            cost_estimate=pl.CostEstimate(flops=12000 * voxels, bytes_accessed=4 * voxels, transcendentals=5 * voxels),
            name=name,
        )(tf_density, tf_color, z1, z2, y1, y2, second, field, *earlier)

    def swapped(value, partner):
        return lax.ppermute(value, "gz", [(i, partner(i)) for i in range(nz)])

    def swapped_first(sent):
        return swapped(sent, lambda i: i ^ 1)

    kept_a, sent_a = render("render_a", 0, split)
    kept_b, sent_b = render("render_b", split, frames - split, kept_a)
    arrived_a, sent_b = lax.optimization_barrier((swapped_first(sent_a), sent_b))

    def second_join(kept, arrived):
        kept, sent = halves(joined(kept, arrived, place % 2 == 0), late)
        return joined(kept, swapped(sent, lambda i: i ^ 2), place // 2 % 2 == 0)

    value = jnp.concatenate([second_join(kept_a, arrived_a), second_join(kept_b, swapped_first(sent_b))], axis=1)
    kept, sent = halves(value, place // 4)
    value = joined(kept, swapped(sent, lambda i: nz - 1 - i), place < nz // 2)[0]
    return jnp.concatenate([value[:, :3], 1.0 - jnp.exp2(value[:, 3:])], axis=1)


def solution(mesh):
    placed = (P(None, "gz", None, "gy"), P(), P())
    return jax.shard_map(
        local, mesh=mesh, in_specs=placed, out_specs=P(None, None, "gz", "gy"), check_vma=False
    )
```

```python
import functools
import math

import jax
import jax.numpy as jnp
from jax import lax
from jax.experimental import pallas as pl
from jax.experimental.pallas import tpu as pltpu
from jax.sharding import PartitionSpec as P

BUMPS = 8
SPACING = 4.0 / (BUMPS - 1)
LOG2E = math.log2(math.e)
LIFT = 49.0
RATE = 4.0 * SPACING * LOG2E
BELL = -2.0 * LOG2E / (RATE * RATE)
LEAN = -8.0 * LOG2E / RATE
FALL = [math.exp(-2.0 * (-2.0 + SPACING * j) ** 2) * 2.0**-LIFT for j in range(BUMPS)]
LANES = 128
TILE = 8
PITCH = 40


def edges_kernel(field_ref, outer_ref, second_ref, pair_ref, next_ref, cells, sems):
    frames, depth, columns = field_ref.shape[:3]
    lane = lax.broadcasted_iota(jnp.int32, (TILE, LANES), 1)
    odd_z = lax.axis_index("gz") % 2 == 1
    spans = [slice(t, t + TILE) for t in range(0, columns, TILE)]

    def load(f):
        return pltpu.make_async_copy(field_ref.at[f], cells.at[f], sems.at[f])

    for f in range(frames):
        load(f).start()

    def one_frame(f, _):
        load(f).wait()
        outer = [jnp.zeros((TILE, LANES), jnp.float32) for _ in spans]
        second = [jnp.zeros((TILE, LANES), jnp.float32) for _ in spans]
        for z in range(depth):
            own = (lane >> 1) == z
            near = (lane == (2 * z - 1) % LANES) | (lane == (2 * z + 2) % LANES)
            for t, span in enumerate(spans):
                turned = pltpu.roll(cells[f, z, span, :], (2 * z + 1) % LANES, 1)
                outer[t] = jnp.where(own, turned, outer[t])
                second[t] = jnp.where(near, turned, second[t])
        for t, span in enumerate(spans):
            outer_ref[f, span, :] = outer[t]
            second_ref[f, span, :] = second[t]
            front, back = cells[f, 0, span, :], cells[f, depth - 1, span, :]
            pair_ref[f, span, :] = jnp.where(odd_z, front, back)
            next_ref[f, span, :] = jnp.where(odd_z, back, front)
        return 0

    lax.fori_loop(0, frames, one_frame, 0)


def quarter_of(place, count):
    return jnp.where(place < count // 2, place, count - 1 - place)


def render_kernel(
    density_ref,
    color_ref,
    z1_ref,
    z2_ref,
    y1_ref,
    y2_ref,
    second_ref,
    field_ref,
    *rest,
    step,
    start,
):
    kept_ref, sent_ref, cells, sems = rest[-4:]
    depth, columns = field_ref.shape[1], field_ref.shape[2]
    frames = kept_ref.shape[1]
    tiles = columns // TILE

    def load(frame, into, t):
        return pltpu.make_async_copy(
            field_ref.at[start + frame, :, pl.ds(t * TILE, TILE), :],
            cells.at[into, pl.ds(1, depth), pl.ds((t + 1) * TILE, TILE), :],
            sems.at[into, t],
        )

    for t in range(tiles):
        load(0, 0, t).start()
    for into in range(2):
        for plane in range(depth + 3):
            cells[into, plane, 0:TILE, :] = jnp.zeros((TILE, LANES), jnp.float32)

    place = lax.axis_index("gz")
    odd_y, odd_z, late = lax.axis_index("gy") % 2 == 1, place % 2 == 1, quarter_of(place, lax.axis_size("gz")) % 2
    lane = lax.broadcasted_iota(jnp.int32, (TILE, LANES), 1)
    even_lane = (lane & 1) == 0
    edge_lane = (lane == 0) | (lane == LANES - 1)
    rows = cells.reshape(2 * cells.shape[1] * PITCH, LANES)
    scale = [-LOG2E * step * FALL[j] for j in range(BUMPS)]
    dens = [jnp.full((TILE, LANES), density_ref[j] * scale[j], jnp.float32) for j in range(BUMPS)]

    def one_tile(frame, slot, t):
        top = slot * (cells.shape[1] * PITCH) + TILE + t * TILE
        here = pl.ds(pl.multiple_of(t * TILE, TILE), TILE)
        a, b = y1_ref[start + frame, here, :], y2_ref[start + frame, here, :]
        left, right = jnp.where(odd_y, a, b), jnp.where(odd_y, b, a)
        second = second_ref[start + frame, here, :]
        rim = jnp.where(
            even_lane,
            pltpu.roll(right, LANES - 1, 1) - pltpu.roll(second, 1, 1),
            pltpu.roll(second, LANES - 1, 1) - pltpu.roll(left, 1, 1),
        )

        def one_depth(z, carry):
            total, clear, before, cell = carry[:4]
            sums = list(carry[4:])
            row = top + (z + 1) * PITCH
            after = rows[pl.ds(pl.multiple_of(row + PITCH, TILE), TILE), :]
            gz = after - before
            gx = rows[pl.ds(row + 1, TILE), :] - rows[pl.ds(row - 1, TILE), :]
            gy = pltpu.roll(cell, LANES - 1, 1) - pltpu.roll(cell, 1, 1)
            gy = jnp.where(edge_lane, pltpu.roll(rim, LANES - 1 - 2 * z, 1), gy)
            slope = jnp.abs(gz + 0.8 * gx + (16.0 / 15.0) * gy)
            lit = (0.3 / 0.42) + slope * lax.rsqrt(gz * gz + gx * gx + gy * gy + 4.0)
            u = cell * RATE
            up = jnp.exp2(u)
            bell = jnp.exp2((u * BELL + LEAN) * u + LIFT)
            series = dens[BUMPS - 1]
            for j in range(BUMPS - 2, -1, -1):
                series = series * up + dens[j]
            total = total + series * bell
            behind = jnp.exp2(total)
            power = (clear - behind) * lit * bell
            sums[0] = sums[0] + power
            for j in range(1, BUMPS):
                power = power * up
                sums[j] = sums[j] + power
            return (total, behind, cell, after, *sums)

        zero = jnp.zeros((TILE, LANES), jnp.float32)
        begin = (
            zero,
            zero + 1.0,
            rows[pl.ds(pl.multiple_of(top, TILE), TILE), :],
            rows[pl.ds(pl.multiple_of(top + PITCH, TILE), TILE), :],
        ) + (zero,) * BUMPS
        final = begin
        for z in range(depth):
            final = one_depth(z, final)
        total, sums = final[0], final[4:]
        parts = []
        for c in range(3):
            parts.append(
                functools.reduce(
                    jnp.add, [(color_ref[c, j] * (0.42 * FALL[j])) * sums[j] for j in range(BUMPS)]
                )
            )
        parts.append(total)
        keep_first = late == jnp.where(t >= 2, 1, 0)
        share = jnp.where(t == 0, 0, jnp.where(t == 1, 2, jnp.where(t == 2, 3, 1)))
        for c in range(4):
            kept_ref[share, frame, c, :, :] = jnp.where(keep_first, parts[c][0:4], parts[c][4:8])
            sent_ref[share, frame, c, :, :] = jnp.where(keep_first, parts[c][4:8], parts[c][0:4])

    def one_frame(frame, _):
        slot = lax.rem(frame, 2)

        @pl.when(frame + 1 < frames)
        def _():
            for t in range(tiles):
                load(frame + 1, 1 - slot, t).start()

        for t in range(tiles):
            here, there = slice(t * TILE, (t + 1) * TILE), slice((t + 1) * TILE, (t + 2) * TILE)
            a, b = z1_ref[start + frame, here, :], z2_ref[start + frame, here, :]
            cells[slot, 0, there, :] = jnp.where(odd_z, a, b)
            cells[slot, depth + 1, there, :] = jnp.where(odd_z, b, a)
        load(frame, slot, 0).wait()

        def with_next(t, _):
            @pl.when(t + 1 < tiles)
            def _():
                load(frame, slot, t + 1).wait()

            one_tile(frame, slot, t)
            return 0

        lax.fori_loop(0, tiles, with_next, 0, unroll=4)
        return 0

    lax.fori_loop(0, frames, one_frame, 0)


def joined(kept, arrived, in_front):
    front, back = jnp.where(in_front, kept, arrived), jnp.where(in_front, arrived, kept)
    clear = jnp.exp2(front[:, :, 3:4])
    return jnp.concatenate([front[:, :, :3] + clear * back[:, :, :3], front[:, :, 3:] + back[:, :, 3:]], axis=2)


def halves(value, late):
    half = value.shape[0] // 2
    kept = jnp.where(late == 0, value[:half], value[half:])
    return kept, jnp.where(late == 0, value[half:], value[:half])


def pairs_of(count, offset):
    lows = range(offset, count - 1, 2)
    return [(i, i + 1) for i in lows] + [(i + 1, i) for i in lows]


def local(field, tf_density, tf_color):
    frames, depth, columns, rows = field.shape
    ny, nz = lax.axis_size("gy"), lax.axis_size("gz")
    step = 1.5 / (depth * nz)
    place = lax.axis_index("gz")
    late = quarter_of(place, nz) // 2
    split = 7

    smem = pl.BlockSpec(memory_space=pltpu.SMEM)
    anywhere, vmem = pl.BlockSpec(memory_space=pl.ANY), pl.BlockSpec(memory_space=pltpu.VMEM)
    plane = jax.ShapeDtypeStruct((frames, columns, rows), jnp.float32)
    outer, second, pair, other = pl.pallas_call(
        edges_kernel,
        in_specs=[anywhere],
        out_specs=[vmem] * 4,
        out_shape=[plane] * 4,
        scratch_shapes=[pltpu.VMEM(field.shape, jnp.float32), pltpu.SemaphoreType.DMA((frames,))],
        compiler_params=pltpu.CompilerParams(vmem_limit_bytes=52 * 2**20),
        name="edges",
    )(field)
    z1 = lax.ppermute(pair, "gz", pairs_of(nz, 0))
    z2 = lax.ppermute(other, "gz", pairs_of(nz, 1))
    y1 = lax.ppermute(outer, "gy", pairs_of(ny, 0))
    y2 = lax.ppermute(outer, "gy", pairs_of(ny, 1))

    def render(name, start, count, *earlier):
        voxels = count * depth * columns * rows
        share = jax.ShapeDtypeStruct((4, count, 4, columns // nz, rows), jnp.float32)
        return pl.pallas_call(
            functools.partial(render_kernel, step=step, start=start),
            in_specs=[smem, smem] + [vmem] * 5 + [anywhere] * (1 + len(earlier)),
            out_specs=[vmem, vmem],
            out_shape=[share, share],
            scratch_shapes=[
                pltpu.VMEM((2, depth + 3, PITCH, LANES), jnp.float32),
                pltpu.SemaphoreType.DMA((2, columns // TILE)),
            ],
            compiler_params=pltpu.CompilerParams(vmem_limit_bytes=52 * 2**20),
            cost_estimate=pl.CostEstimate(flops=12000 * voxels, bytes_accessed=4 * voxels, transcendentals=5 * voxels),
            name=name,
        )(tf_density, tf_color, z1, z2, y1, y2, second, field, *earlier)

    def swapped(value, partner):
        return lax.ppermute(value, "gz", [(i, partner(i)) for i in range(nz)])

    def swapped_first(sent):
        return swapped(sent, lambda i: i ^ 1)

    kept_a, sent_a = render("render_a", 0, split)
    kept_b, sent_b = render("render_b", split, frames - split, kept_a)
    arrived_a, sent_b = lax.optimization_barrier((swapped_first(sent_a), sent_b))

    def second_join(kept, arrived):
        kept, sent = halves(joined(kept, arrived, place % 2 == 0), late)
        return joined(kept, swapped(sent, lambda i: i ^ 2), place // 2 % 2 == 0)

    value = jnp.concatenate([second_join(kept_a, arrived_a), second_join(kept_b, swapped_first(sent_b))], axis=1)
    kept, sent = halves(value, place // 4)
    value = joined(kept, swapped(sent, lambda i: nz - 1 - i), place < nz // 2)[0]
    return jnp.concatenate([value[:, :3], 1.0 - jnp.exp2(value[:, 3:])], axis=1)


def solution(mesh):
    placed = (P(None, "gz", None, "gy"), P(), P())
    return jax.shard_map(
        local, mesh=mesh, in_specs=placed, out_specs=P(None, None, "gz", "gy"), check_vma=False
    )
```

```python
import functools
import math

import jax
import jax.numpy as jnp
from jax import lax
from jax.experimental import pallas as pl
from jax.experimental.pallas import tpu as pltpu
from jax.sharding import PartitionSpec as P

BUMPS = 8
SPACING = 4.0 / (BUMPS - 1)
LOG2E = math.log2(math.e)
LIFT = 49.0
RATE = 4.0 * SPACING * LOG2E
BELL = -2.0 * LOG2E / (RATE * RATE)
LEAN = -8.0 * LOG2E / RATE
FALL = [math.exp(-2.0 * (-2.0 + SPACING * j) ** 2) * 2.0**-LIFT for j in range(BUMPS)]
LANES = 128
TILE = 8
PITCH = 40


def edges_kernel(field_ref, outer_ref, second_ref, pair_ref, next_ref, cells, sems):
    frames, depth, columns = field_ref.shape[:3]
    lane = lax.broadcasted_iota(jnp.int32, (TILE, LANES), 1)
    odd_z = lax.axis_index("gz") % 2 == 1
    spans = [slice(t, t + TILE) for t in range(0, columns, TILE)]

    def load(f):
        return pltpu.make_async_copy(field_ref.at[f], cells.at[f], sems.at[f])

    for f in range(frames):
        load(f).start()

    def one_frame(f, _):
        load(f).wait()
        outer = [jnp.zeros((TILE, LANES), jnp.float32) for _ in spans]
        second = [jnp.zeros((TILE, LANES), jnp.float32) for _ in spans]
        for z in range(depth):
            own = (lane >> 1) == z
            near = (lane == (2 * z - 1) % LANES) | (lane == (2 * z + 2) % LANES)
            for t, span in enumerate(spans):
                turned = pltpu.roll(cells[f, z, span, :], (2 * z + 1) % LANES, 1)
                outer[t] = jnp.where(own, turned, outer[t])
                second[t] = jnp.where(near, turned, second[t])
        for t, span in enumerate(spans):
            outer_ref[f, span, :] = outer[t]
            second_ref[f, span, :] = second[t]
            front, back = cells[f, 0, span, :], cells[f, depth - 1, span, :]
            pair_ref[f, span, :] = jnp.where(odd_z, front, back)
            next_ref[f, span, :] = jnp.where(odd_z, back, front)
        return 0

    lax.fori_loop(0, frames, one_frame, 0)


def quarter_of(place, count):
    return jnp.where(place < count // 2, place, count - 1 - place)


def render_kernel(
    density_ref,
    color_ref,
    z1_ref,
    z2_ref,
    y1_ref,
    y2_ref,
    second_ref,
    field_ref,
    *rest,
    step,
    start,
):
    kept_ref, sent_ref, cells, sems = rest[-4:]
    depth, columns = field_ref.shape[1], field_ref.shape[2]
    frames = kept_ref.shape[1]
    tiles = columns // TILE

    def load(frame, into, t):
        return pltpu.make_async_copy(
            field_ref.at[start + frame, :, pl.ds(t * TILE, TILE), :],
            cells.at[into, pl.ds(1, depth), pl.ds((t + 1) * TILE, TILE), :],
            sems.at[into, t],
        )

    for t in range(tiles):
        load(0, 0, t).start()
    for into in range(2):
        for plane in range(depth + 3):
            cells[into, plane, 0:TILE, :] = jnp.zeros((TILE, LANES), jnp.float32)

    place = lax.axis_index("gz")
    odd_y, odd_z, late = lax.axis_index("gy") % 2 == 1, place % 2 == 1, quarter_of(place, lax.axis_size("gz")) % 2
    lane = lax.broadcasted_iota(jnp.int32, (TILE, LANES), 1)
    even_lane = (lane & 1) == 0
    edge_lane = (lane == 0) | (lane == LANES - 1)
    rows = cells.reshape(2 * cells.shape[1] * PITCH, LANES)
    scale = [-LOG2E * step * FALL[j] for j in range(BUMPS)]
    dens = [jnp.full((TILE, LANES), density_ref[j] * scale[j], jnp.float32) for j in range(BUMPS)]

    def one_tile(frame, slot, t):
        top = slot * (cells.shape[1] * PITCH) + TILE + t * TILE
        here = pl.ds(pl.multiple_of(t * TILE, TILE), TILE)
        a, b = y1_ref[start + frame, here, :], y2_ref[start + frame, here, :]
        left, right = jnp.where(odd_y, a, b), jnp.where(odd_y, b, a)
        second = second_ref[start + frame, here, :]
        rim = jnp.where(
            even_lane,
            pltpu.roll(right, LANES - 1, 1) - pltpu.roll(second, 1, 1),
            pltpu.roll(second, LANES - 1, 1) - pltpu.roll(left, 1, 1),
        )

        def one_depth(z, carry):
            total, clear, before, cell = carry[:4]
            sums = list(carry[4:])
            row = top + (z + 1) * PITCH
            after = rows[pl.ds(pl.multiple_of(row + PITCH, TILE), TILE), :]
            gz = after - before
            gx = rows[pl.ds(row + 1, TILE), :] - rows[pl.ds(row - 1, TILE), :]
            gy = pltpu.roll(cell, LANES - 1, 1) - pltpu.roll(cell, 1, 1)
            gy = jnp.where(edge_lane, pltpu.roll(rim, LANES - 1 - 2 * z, 1), gy)
            slope = jnp.abs(gz + 0.8 * gx + (16.0 / 15.0) * gy)
            lit = (0.3 / 0.42) + slope * lax.rsqrt(gz * gz + gx * gx + gy * gy + 4.0)
            u = cell * RATE
            up = jnp.exp2(u)
            bell = jnp.exp2((u * BELL + LEAN) * u + LIFT)
            series = dens[BUMPS - 1]
            for j in range(BUMPS - 2, -1, -1):
                series = series * up + dens[j]
            total = total + series * bell
            behind = jnp.exp2(total)
            power = (clear - behind) * lit * bell
            sums[0] = sums[0] + power
            for j in range(1, BUMPS):
                power = power * up
                sums[j] = sums[j] + power
            return (total, behind, cell, after, *sums)

        zero = jnp.zeros((TILE, LANES), jnp.float32)
        begin = (
            zero,
            zero + 1.0,
            rows[pl.ds(pl.multiple_of(top, TILE), TILE), :],
            rows[pl.ds(pl.multiple_of(top + PITCH, TILE), TILE), :],
        ) + (zero,) * BUMPS
        final = begin
        for z in range(depth):
            final = one_depth(z, final)
        total, sums = final[0], final[4:]
        parts = []
        for c in range(3):
            parts.append(
                functools.reduce(
                    jnp.add, [(color_ref[c, j] * (0.42 * FALL[j])) * sums[j] for j in range(BUMPS)]
                )
            )
        parts.append(total)
        keep_first = late == jnp.where(t >= 2, 1, 0)
        share = jnp.where(t == 0, 0, jnp.where(t == 1, 2, jnp.where(t == 2, 3, 1)))
        for c in range(4):
            kept_ref[share, frame, c, :, :] = jnp.where(keep_first, parts[c][0:4], parts[c][4:8])
            sent_ref[share, frame, c, :, :] = jnp.where(keep_first, parts[c][4:8], parts[c][0:4])

    def one_frame(frame, _):
        slot = lax.rem(frame, 2)

        for t in range(tiles):
            here, there = slice(t * TILE, (t + 1) * TILE), slice((t + 1) * TILE, (t + 2) * TILE)
            a, b = z1_ref[start + frame, here, :], z2_ref[start + frame, here, :]
            cells[slot, 0, there, :] = jnp.where(odd_z, a, b)
            cells[slot, depth + 1, there, :] = jnp.where(odd_z, b, a)
        load(frame, slot, 0).wait()

        @pl.when(frame + 1 < frames)
        def _():
            for t in range(tiles):
                load(frame + 1, 1 - slot, t).start()

        def with_next(t, _):
            @pl.when(t + 1 < tiles)
            def _():
                load(frame, slot, t + 1).wait()

            one_tile(frame, slot, t)
            return 0

        lax.fori_loop(0, tiles, with_next, 0, unroll=4)
        return 0

    lax.fori_loop(0, frames, one_frame, 0)


def joined(kept, arrived, in_front):
    front, back = jnp.where(in_front, kept, arrived), jnp.where(in_front, arrived, kept)
    clear = jnp.exp2(front[:, :, 3:4])
    return jnp.concatenate([front[:, :, :3] + clear * back[:, :, :3], front[:, :, 3:] + back[:, :, 3:]], axis=2)


def halves(value, late):
    half = value.shape[0] // 2
    kept = jnp.where(late == 0, value[:half], value[half:])
    return kept, jnp.where(late == 0, value[half:], value[:half])


def pairs_of(count, offset):
    lows = range(offset, count - 1, 2)
    return [(i, i + 1) for i in lows] + [(i + 1, i) for i in lows]


def local(field, tf_density, tf_color):
    frames, depth, columns, rows = field.shape
    ny, nz = lax.axis_size("gy"), lax.axis_size("gz")
    step = 1.5 / (depth * nz)
    place = lax.axis_index("gz")
    late = quarter_of(place, nz) // 2
    split = 7

    smem = pl.BlockSpec(memory_space=pltpu.SMEM)
    anywhere, vmem = pl.BlockSpec(memory_space=pl.ANY), pl.BlockSpec(memory_space=pltpu.VMEM)
    plane = jax.ShapeDtypeStruct((frames, columns, rows), jnp.float32)
    outer, second, pair, other = pl.pallas_call(
        edges_kernel,
        in_specs=[anywhere],
        out_specs=[vmem] * 4,
        out_shape=[plane] * 4,
        scratch_shapes=[pltpu.VMEM(field.shape, jnp.float32), pltpu.SemaphoreType.DMA((frames,))],
        compiler_params=pltpu.CompilerParams(vmem_limit_bytes=52 * 2**20),
        name="edges",
    )(field)
    z1 = lax.ppermute(pair, "gz", pairs_of(nz, 0))
    z2 = lax.ppermute(other, "gz", pairs_of(nz, 1))
    y1 = lax.ppermute(outer, "gy", pairs_of(ny, 0))
    y2 = lax.ppermute(outer, "gy", pairs_of(ny, 1))

    def render(name, start, count, *earlier):
        voxels = count * depth * columns * rows
        share = jax.ShapeDtypeStruct((4, count, 4, columns // nz, rows), jnp.float32)
        return pl.pallas_call(
            functools.partial(render_kernel, step=step, start=start),
            in_specs=[smem, smem] + [vmem] * 5 + [anywhere] * (1 + len(earlier)),
            out_specs=[vmem, vmem],
            out_shape=[share, share],
            scratch_shapes=[
                pltpu.VMEM((2, depth + 3, PITCH, LANES), jnp.float32),
                pltpu.SemaphoreType.DMA((2, columns // TILE)),
            ],
            compiler_params=pltpu.CompilerParams(vmem_limit_bytes=52 * 2**20),
            cost_estimate=pl.CostEstimate(flops=12000 * voxels, bytes_accessed=4 * voxels, transcendentals=5 * voxels),
            name=name,
        )(tf_density, tf_color, z1, z2, y1, y2, second, field, *earlier)

    def swapped(value, partner):
        return lax.ppermute(value, "gz", [(i, partner(i)) for i in range(nz)])

    def swapped_first(sent):
        return swapped(sent, lambda i: i ^ 1)

    kept_a, sent_a = render("render_a", 0, split)
    kept_b, sent_b = render("render_b", split, frames - split, kept_a)
    arrived_a, sent_b = lax.optimization_barrier((swapped_first(sent_a), sent_b))

    def second_join(kept, arrived):
        kept, sent = halves(joined(kept, arrived, place % 2 == 0), late)
        return joined(kept, swapped(sent, lambda i: i ^ 2), place // 2 % 2 == 0)

    value = jnp.concatenate([second_join(kept_a, arrived_a), second_join(kept_b, swapped_first(sent_b))], axis=1)
    kept, sent = halves(value, place // 4)
    value = joined(kept, swapped(sent, lambda i: nz - 1 - i), place < nz // 2)[0]
    return jnp.concatenate([value[:, :3], 1.0 - jnp.exp2(value[:, 3:])], axis=1)


def solution(mesh):
    placed = (P(None, "gz", None, "gy"), P(), P())
    return jax.shard_map(
        local, mesh=mesh, in_specs=placed, out_specs=P(None, None, "gz", "gy"), check_vma=False
    )
```
